256 devices in a mesh: ctx: 16 (over y, x_lo, core), tp: 16 (over z, x_hi).
Axes of the slice: x: 4 (x_hi: 2, x_lo: 2; x = x_hi * 2 + x_lo), y: 4, z: 8, core: 2. Of those that a mesh axis runs over, the one named last changes fastest.
Arguments:
- queries: bfloat16 [4096, 64, 128], P('ctx', 'tp'), may hold values from -7.5 to 7.5
- key_vectors: bfloat16 [4096, 8, 128], P('ctx'), may hold values from -7.5 to 7.5
- value_vectors: bfloat16 [4096, 8, 128], P('ctx'), may hold values from -6 to 6
- out_grad: bfloat16 [4096, 64, 128], P('ctx', 'tp'), may hold values from -6 to 6
- doc_ids: int32 [4096], P('ctx'), may hold values from 0 to 15, never falling along the last dimension, each value on 1 to 2048 neighbouring positions
Outputs:
- attended: bfloat16 [4096, 64, 128], P('ctx', 'tp')
- query_grad: bfloat16 [4096, 64, 128], P('ctx', 'tp')
- key_grad: bfloat16 [4096, 8, 128], P('ctx')
- value_grad: bfloat16 [4096, 8, 128], P('ctx')
The draws below stay inside these ranges and needn't reach their ends.
Inputs may be any that keep to these rules, and one draw needn't show every extreme that they name: `doc_ids`: document ids never fall along the tokens; each document is a run of at most 2048 tokens, and one has exactly that many.
All inputs are finite; a program needn't handle non-finite values.
Results may differ from the reference program's by a relative error of at most 0.019.
Values may be sent and summed in bfloat16 or wider, within the bound.
No kernel may reach another device: no remote copies, remote signals or barrier semaphores. Data moves between devices by JAX's collectives and lax.ppermute only.
A program may use at most 64 MiB of HBM per device.

```python
import math
import jax
import jax.numpy as jnp
import numpy as np
from jax import lax

QH = 64
KVH = 8
HD = 128
DOCS = 16
TOKENS = 4096


def draw_queries(key, part):
    key = jax.random.fold_in(key, 21)
    first_key = jax.random.fold_in(key, 0)
    return jnp.clip(jax.random.normal(first_key, (TOKENS, QH, HD), jnp.float32), -6.0, 6.0).astype(jnp.bfloat16)


def draw_key_vectors(key, part):
    key = jax.random.fold_in(key, 37)
    first_key = jax.random.fold_in(key, 0)
    return jnp.clip(jax.random.normal(first_key, (TOKENS, KVH, HD), jnp.float32), -6.0, 6.0).astype(jnp.bfloat16)


def level_of(stream_key, shape, pieces, low, largest):
    def one(position, shards_of):
        draws = jax.random.uniform(jax.random.fold_in(jax.random.fold_in(stream_key, 6), position), (shards_of,), jnp.float32, low / len(pieces), largest / len(pieces))
        return jnp.repeat(jnp.exp(draws), shape[position] // shards_of).reshape((-1,) + (1,) * (len(shape) - position - 1))

    gain = one(*pieces[0])
    for cut in pieces[1:]:
        gain = gain * one(*cut)
    return gain


def profile(number_of, total, reach, slope):
    portions = [(1 << 20) // math.isqrt(grade ** slope) + 1 for grade in range(2, number_of + 1)]
    spare, given = total - reach - (number_of - 1), [1] * (number_of - 1)
    while spare > 0:
        movable = [i for i in range(number_of - 1) if given[i] < reach]
        pool, left = sum([portions[i] for i in movable]), spare
        for i in movable:
            addition = min(reach - given[i], max(1, left * portions[i] // pool), spare)
            given[i] = given[i] + addition
            spare = spare - addition
    return np.array([reach] + given)


def uneven(stream_key, number_of, total, reach, skew):
    if number_of == 2:
        one = jax.random.randint(stream_key, (), max(1, total - reach), min(reach, total - 1) + 1)
        return jnp.stack([one, total - one])
    sizes = jnp.asarray(profile(number_of, total, reach, skew), jnp.int32)
    pairs = (number_of - 1) // 2
    giver, receiver = sizes[1:1 + 2 * pairs:2], sizes[2:2 + 2 * pairs:2]
    slack = jnp.minimum(giver - 1, reach - receiver)
    passed = jax.random.randint(jax.random.fold_in(stream_key, 1), (pairs,), 0, 1 << 20) % (slack + 1)
    sizes = sizes.at[1:1 + 2 * pairs:2].set(giver - passed).at[2:2 + 2 * pairs:2].set(receiver + passed)
    return sizes[jax.random.permutation(jax.random.fold_in(stream_key, 2), number_of)]


def bell_draw(own_key, shape, deviation, reach, shards=(), held_as=jnp.bfloat16):
    drawn = jax.random.normal(own_key, shape, jnp.float32) * deviation
    if len(shards) > 0:
        drawn = level_of(own_key, shape, shards, -0.22, 0.18) * drawn
    return jnp.clip(drawn, min=-reach, max=reach).astype(held_as)


def setup_inputs(seed: int = 0) -> dict:
    arg_keys = jax.random.split(jax.random.key(seed), 6)
    return {
        "queries": draw_queries(jax.random.fold_in(arg_keys[5], 71), 0),
        "key_vectors": draw_key_vectors(jax.random.fold_in(arg_keys[5], 71), 0),
        "value_vectors": bell_draw(arg_keys[2], (TOKENS, KVH, HD), 1.0, 6.0, ((0, 16),)),
        "out_grad": bell_draw(arg_keys[3], (TOKENS, QH, HD), 1.0, 6.0, ((0, 16), (1, 16))),
        "doc_ids": jnp.searchsorted(jnp.cumsum(uneven(arg_keys[4], DOCS, TOKENS, TOKENS // 2, 0)), jnp.arange(TOKENS), side="right").astype(jnp.int32),
    }


NEGATIVE = -1e+30

def reference(queries, key_vectors, value_vectors, out_grad, doc_ids):
    group_size = QH // KVH
    factor = 1.0 / math.sqrt(HD)
    span_rows = math.gcd(TOKENS, 512)
    num_blocks = TOKENS // span_rows
    positions = jnp.arange(TOKENS, dtype=jnp.int32)
    grouped_q = jnp.transpose(queries.reshape(TOKENS, KVH, group_size, HD), (1, 0, 2, 3))
    grouped_g = jnp.transpose(out_grad.reshape(TOKENS, KVH, group_size, HD), (1, 0, 2, 3))
    per_key = jnp.transpose(key_vectors, (1, 0, 2))
    per_value = jnp.transpose(value_vectors, (1, 0, 2))

    def one_head(operands):
        head_q, head_k, head_v, head_g = operands
        key_float = head_k.astype(jnp.float32)
        value_float = head_v.astype(jnp.float32)

        def masked_scores(block_index):
            start = (block_index * span_rows).astype(jnp.int32)
            query_rows = lax.dynamic_slice_in_dim(head_q, start, span_rows, 0).astype(jnp.float32)
            row_pos = lax.dynamic_slice_in_dim(positions, start, span_rows, 0)
            row_doc = lax.dynamic_slice_in_dim(doc_ids, start, span_rows, 0)
            scores = jnp.einsum('igd,jd->gij', query_rows, key_float) * factor
            allowed = (positions[None, :] <= row_pos[:, None]) & (doc_ids[None, :] == row_doc[:, None])
            return (query_rows, scores, allowed)

        def forward_block(block_index):
            query_rows, scores, allowed = masked_scores(block_index)
            running_max = lax.optimization_barrier(jnp.max(jnp.where(allowed, scores, NEGATIVE), axis=2))
            weights = jnp.where(allowed, jnp.exp(scores - running_max[..., None]), 0.0)
            row_mass = lax.optimization_barrier(jnp.sum(weights, axis=2))
            rounded = weights.astype(jnp.bfloat16).astype(jnp.float32)
            summed = jnp.einsum('gij,jd->igd', rounded, value_float)
            result = (summed / jnp.transpose(row_mass)[..., None]).astype(jnp.bfloat16)
            return (result, running_max + jnp.log(row_mass))
        indices = jnp.arange(num_blocks, dtype=jnp.int32)
        result, log_total = lax.map(forward_block, indices)
        result = result.reshape(TOKENS, group_size, HD)
        row_delta = lax.optimization_barrier(jnp.sum(head_g.astype(jnp.float32) * result.astype(jnp.float32), axis=2))

        def backward_block(carried, block_index):
            key_acc, value_acc = carried
            query_rows, scores, allowed = masked_scores(block_index)
            start = (block_index * span_rows).astype(jnp.int32)
            grad_rows = lax.dynamic_slice_in_dim(head_g, start, span_rows, 0).astype(jnp.float32)
            delta_rows = jnp.transpose(lax.dynamic_slice_in_dim(row_delta, start, span_rows, 0))
            row_lse = log_total[block_index]
            probability = jnp.where(allowed, jnp.exp(scores - row_lse[..., None]), 0.0)
            value_acc = value_acc + jnp.einsum('gij,igd->jd', probability.astype(jnp.bfloat16).astype(jnp.float32), grad_rows)
            prob_grad = jnp.einsum('igd,jd->gij', grad_rows, value_float)
            score_grad = (probability * (prob_grad - delta_rows[..., None])).astype(jnp.bfloat16).astype(jnp.float32)
            query_grad = (jnp.einsum('gij,jd->igd', score_grad, key_float) * factor).astype(jnp.bfloat16)
            key_acc = key_acc + jnp.einsum('gij,igd->jd', score_grad, query_rows)
            return ((key_acc, value_acc), query_grad)
        blank_rows = jnp.zeros((TOKENS, HD), jnp.float32)
        (key_acc, value_acc), query_grad = lax.scan(backward_block, (blank_rows, blank_rows), indices)
        return (result, query_grad.reshape(TOKENS, group_size, HD), (key_acc * factor).astype(jnp.bfloat16), value_acc.astype(jnp.bfloat16))
    outputs = lax.map(one_head, (grouped_q, per_key, per_value, grouped_g))
    attended = jnp.transpose(outputs[0], (1, 0, 2, 3)).reshape(TOKENS, QH, HD)
    query_grad = jnp.transpose(outputs[1], (1, 0, 2, 3)).reshape(TOKENS, QH, HD)
    key_grad = jnp.transpose(outputs[2], (1, 0, 2))
    value_grad = jnp.transpose(outputs[3], (1, 0, 2))
    return (attended, query_grad, key_grad, value_grad)
```

```python
import functools
import math

import jax
import jax.numpy as jnp
from jax import lax
from jax.experimental import pallas as pl
from jax.experimental.pallas import tpu as pltpu
from jax.sharding import PartitionSpec as P

KVH = 8
NEGATIVE = -1e30
BACK = 4
F32 = jnp.float32
BF16 = jnp.bfloat16


def dot(a, b, contract):
    return lax.dot_general(a, b, ((contract[:1], contract[1:]), ((), ())), preferred_element_type=F32)


def attention_kernel(
    core_ref, q_ref, g_ref, mine_ref, sib_ref,
    att_ref, dq_ref, dmine_ref, dsib_ref,
    s_ref, o_ref, acc_ref,
):
    heads, rows, width = q_ref.shape
    blocks = mine_ref.shape[0]
    factor = 1.0 / math.sqrt(width)
    base2 = factor / math.log(2.0)
    core = core_ref[0]
    sources = ((mine_ref, dmine_ref, core), (sib_ref, dsib_ref, 1 - core))
    q_doc = mine_ref[blocks - 1, pl.ds(rows, 16), :].astype(F32)[:1]
    key_iota = lax.broadcasted_iota(jnp.int32, (rows, rows), 0)
    row_iota = lax.broadcasted_iota(jnp.int32, (rows, rows), 1)

    def scores_step(a, peaks):
        peaks = list(peaks)
        for s, (ref, _, side) in enumerate(sources):
            keys = ref[a, pl.ds(0, rows), pl.ds(0, width)]
            k_doc = ref[a, pl.ds(rows, 16), :].astype(F32)[:1]
            k_col = jnp.transpose(jnp.broadcast_to(k_doc, (width, rows)))
            k_col = jnp.concatenate([k_col] * (rows // width), axis=1)
            ahead = (2 * (a - (blocks - 1)) + side - core) * rows
            allowed = (k_col == q_doc) & (key_iota + ahead <= row_iota)
            for h in range(heads):
                raw = jnp.where(allowed, dot(keys, q_ref[h], (1, 1)), NEGATIVE)
                s_ref[a, s, h] = raw
                peaks[h] = jnp.maximum(peaks[h], jnp.max(raw.reshape(rows // 8, 8, rows), axis=0))
        return tuple(peaks)

    peaks = lax.fori_loop(
        0, blocks, scores_step, tuple(jnp.full((8, rows), NEGATIVE, F32) for _ in range(heads))
    )
    peak = [jnp.max(p, axis=0, keepdims=True) for p in peaks]
    o_ref[...] = jnp.zeros_like(o_ref)

    def weights_step(a, masses):
        masses = list(masses)
        for s, (ref, _, _) in enumerate(sources):
            values = ref[a, pl.ds(0, rows), pl.ds(width, width)]
            for h in range(heads):
                weights = jnp.exp2((s_ref[a, s, h] - peak[h]) * base2)
                s_ref[a, s, h] = weights
                masses[h] = masses[h] + jnp.sum(weights.reshape(rows // 8, 8, rows), axis=0)
                o_ref[h] += dot(values, weights.astype(BF16), (0, 0))
        return tuple(masses)

    masses = lax.fori_loop(
        0, blocks, weights_step, tuple(jnp.zeros((8, rows), F32) for _ in range(heads))
    )
    inverse, delta = [], []
    for h in range(heads):
        mass = jnp.sum(masses[h], axis=0, keepdims=True)
        inverse.append(1.0 / mass)
        out = (o_ref[h] / mass).astype(BF16).astype(F32)
        grad = jnp.transpose(g_ref[h].astype(F32))
        delta.append(jnp.sum(out * grad, axis=0, keepdims=True))
        att_ref[h] = jnp.transpose(out).astype(BF16)
    acc_ref[...] = jnp.zeros_like(acc_ref)

    def grads_step(a, carried):
        for s, (ref, out_ref, _) in enumerate(sources):
            keys = ref[a, pl.ds(0, rows), pl.ds(0, width)]
            values = ref[a, pl.ds(0, rows), pl.ds(width, width)]
            d_keys = jnp.zeros((rows, width), F32)
            d_values = jnp.zeros((rows, width), F32)
            for h in range(heads):
                prob = s_ref[a, s, h] * inverse[h]
                d_values += dot(prob.astype(BF16), g_ref[h], (1, 0))
                d_prob = dot(values, g_ref[h], (1, 1))
                d_score = (prob * (d_prob - delta[h])).astype(BF16)
                d_keys += dot(d_score, q_ref[h], (1, 0))
                acc_ref[h] += dot(keys, d_score, (0, 0))
            out_ref[a, :, pl.ds(0, width)] = (d_keys * factor).astype(BF16)
            out_ref[a, :, pl.ds(width, width)] = d_values.astype(BF16)
        return carried

    lax.fori_loop(0, blocks, grads_step, 0)
    for h in range(heads):
        dq_ref[h] = (jnp.transpose(acc_ref[h]) * factor).astype(BF16)


def attention(core, q, g, mine, sib):
    heads, rows, width = q.shape
    blocks = mine.shape[0]
    vmem = pl.BlockSpec(memory_space=pltpu.VMEM)
    shape = jax.ShapeDtypeStruct
    return pl.pallas_call(
        attention_kernel,
        out_shape=(
            shape((heads, rows, width), BF16),
            shape((heads, rows, width), BF16),
            shape((blocks, rows, 2 * width), BF16),
            shape((blocks, rows, 2 * width), BF16),
        ),
        in_specs=[pl.BlockSpec(memory_space=pltpu.SMEM)] + [vmem] * 4,
        out_specs=(vmem,) * 4,
        scratch_shapes=[
            pltpu.VMEM((blocks, 2, heads, rows, rows), F32),
            pltpu.VMEM((heads, width, rows), F32),
            pltpu.VMEM((heads, width, rows), F32),
        ],
        compiler_params=pltpu.CompilerParams(vmem_limit_bytes=40 * 1024 * 1024),
        name="attention",
    )(core, q, g, mine, sib)


def per_device(queries, key_vectors, value_vectors, out_grad, doc_ids):
    rows, heads, width = queries.shape
    ctx_count = lax.axis_size("ctx")
    tp_count = lax.axis_size("tp")
    ctx_rank = lax.axis_index("ctx")
    tp_rank = lax.axis_index("tp")
    share = tp_count // KVH
    kv_head = tp_rank // share
    half = lax.rem(tp_rank, share)
    core = lax.rem(ctx_rank, 2).reshape(1)
    swap_core = [(i, i ^ 1) for i in range(ctx_count)]
    swap_half = [(i, i ^ 1) for i in range(tp_count)]

    def head_of(array):
        return lax.dynamic_slice_in_dim(array, kv_head, 1, 1).reshape(rows, width)

    doc_rows = jnp.broadcast_to((doc_ids + 1).astype(BF16)[None], (16, rows))
    pair = jnp.concatenate([head_of(key_vectors), head_of(value_vectors)], axis=1)
    own = jnp.concatenate([pair, doc_rows], axis=0)
    parts = [
        lax.ppermute(own, "ctx", [(i, i + 2 * d) for i in range(ctx_count - 2 * d)])
        for d in range(BACK, 0, -1)
    ]
    mine = jnp.stack(parts + [own])
    sib = lax.ppermute(mine, "ctx", swap_core)
    q = jnp.transpose(queries, (1, 0, 2))
    g = jnp.transpose(out_grad, (1, 0, 2))
    att, dq, d_mine, d_sib = attention(core, q, g, mine, sib)

    from_sib = lax.ppermute(d_sib, "ctx", swap_core)
    both = [(d_mine[a].astype(F32) + from_sib[a].astype(F32)) for a in range(BACK + 1)]
    total = both[BACK]
    for a in range(BACK):
        d = BACK - a
        total = total + lax.ppermute(
            both[a].astype(BF16), "ctx", [(i, i - 2 * d) for i in range(2 * d, ctx_count)]
        ).astype(F32)
    part = rows // share
    kept = lax.dynamic_slice_in_dim(total, half * part, part, 0)
    given = lax.dynamic_slice_in_dim(total, (1 - half) * part, part, 0).astype(BF16)
    final = (kept + lax.ppermute(given, "tp", swap_half).astype(F32)).astype(BF16)

    around = [final] + [
        lax.ppermute(final, "tp", [(i, (i + share * d) % tp_count) for i in range(tp_count)])
        for d in range(1, KVH)
    ]
    near = jnp.stack(around[::-1])
    far = lax.ppermute(near, "tp", swap_half)
    halves = jnp.where(half == 0, jnp.stack([near, far]), jnp.stack([far, near]))
    ring = jnp.concatenate([halves, halves], axis=1)
    ordered = lax.dynamic_slice_in_dim(ring, KVH - 1 - kv_head, KVH, 1)
    merged = jnp.transpose(ordered, (0, 2, 1, 3)).reshape(rows, KVH, 2 * width)
    return (
        jnp.transpose(att, (1, 0, 2)),
        jnp.transpose(dq, (1, 0, 2)),
        merged[:, :, :width],
        merged[:, :, width:],
    )


def solution(mesh):
    return jax.shard_map(
        per_device,
        mesh=mesh,
        in_specs=(
            P("ctx", "tp", None),
            P("ctx", None, None),
            P("ctx", None, None),
            P("ctx", "tp", None),
            P("ctx"),
        ),
        out_specs=(
            P("ctx", "tp", None),
            P("ctx", "tp", None),
            P("ctx", None, None),
            P("ctx", None, None),
        ),
        check_vma=False,
    )
```

```python
import functools
import math

import jax
import jax.numpy as jnp
from jax import lax
from jax.experimental import pallas as pl
from jax.experimental.pallas import tpu as pltpu
from jax.sharding import PartitionSpec as P

KVH = 8
NEGATIVE = -1e30
BACK = 4
F32 = jnp.float32
BF16 = jnp.bfloat16


def dot(a, b, contract=(1, 0)):
    return lax.dot_general(a, b, ((contract[:1], contract[1:]), ((), ())), preferred_element_type=F32)


def attention_kernel(
    core_ref, q_ref, g_ref, mine_ref, sib_ref,
    att_ref, dq_ref, dmine_ref, dsib_ref,
    s_ref, p_ref, ds_ref, o_ref, qt_ref, gt_ref, kt_ref, vt_ref,
):
    heads, rows, width = q_ref.shape
    last = mine_ref.shape[0] - 1
    factor = 1.0 / math.sqrt(width)
    base2 = factor / math.log(2.0)
    core = core_ref[0]
    q_doc = mine_ref[last, pl.ds(rows, 16), :].astype(F32)[:1]
    for h in range(heads):
        qt_ref[h] = jnp.transpose(q_ref[h])
        gt_ref[h] = jnp.transpose(g_ref[h])

    def earlier(j):
        return (2 * j, mine_ref, dmine_ref, j), (2 * j + 1, sib_ref, dsib_ref, j + core)

    own = ((2 * last, mine_ref, dmine_ref, last),)

    def sweep(step, start):
        carried = lax.fori_loop(0, last, lambda j, c: step(earlier(j), c), start)
        return step(own, carried)

    def columns(n):
        return pl.ds(pl.multiple_of(n * rows, rows), rows)

    def scores_step(blocks, peaks):
        peaks = list(peaks)
        for n, ref, _, a in blocks:
            keys = ref[a, pl.ds(0, rows), pl.ds(0, width)]
            k_doc = ref[a, pl.ds(rows, 16), :].astype(F32)[:1]
            k_col = jnp.transpose(jnp.broadcast_to(k_doc, (width, rows)))
            allowed = jnp.concatenate([k_col] * (rows // width), axis=1) == q_doc
            if blocks is own:
                allowed &= lax.broadcasted_iota(jnp.int32, (rows, rows), 0) <= (
                    lax.broadcasted_iota(jnp.int32, (rows, rows), 1)
                )
            for h in range(heads):
                raw = jnp.where(allowed, dot(keys, qt_ref[h]), NEGATIVE)
                s_ref[n, h] = raw
                peaks[h] = jnp.maximum(peaks[h], jnp.max(raw.reshape(rows // 8, 8, rows), axis=0))
        return tuple(peaks)

    peaks = sweep(scores_step, tuple(jnp.full((8, rows), NEGATIVE, F32) for _ in range(heads)))
    peak = [jnp.max(p, axis=0, keepdims=True) for p in peaks]

    def weights_step(blocks, masses):
        masses = list(masses)
        for n, ref, _, a in blocks:
            vt_ref[:, columns(n)] = jnp.transpose(ref[a, pl.ds(0, rows), pl.ds(width, width)])
            for h in range(heads):
                weights = jnp.exp2((s_ref[n, h] - peak[h]) * base2)
                s_ref[n, h] = weights
                masses[h] = masses[h] + jnp.sum(weights.reshape(rows // 8, 8, rows), axis=0)
                p_ref[n, :, pl.ds(h * rows, rows)] = weights.astype(BF16)
        return tuple(masses)

    masses = sweep(weights_step, tuple(jnp.zeros((8, rows), F32) for _ in range(heads)))
    inverse, delta = [], []
    for h in range(heads):
        mass = jnp.sum(masses[h], axis=0, keepdims=True)
        inverse.append(1.0 / mass)
        weights = p_ref[:, :, pl.ds(h * rows, rows)].reshape(-1, rows)
        out = (dot(vt_ref[...], weights) / mass).astype(BF16).astype(F32)
        delta.append(jnp.sum(out * gt_ref[h].astype(F32), axis=0, keepdims=True))
        o_ref[h] = out

    def score_grads_step(blocks, carried):
        for n, ref, _, a in blocks:
            values = ref[a, pl.ds(0, rows), pl.ds(width, width)]
            kt_ref[:, columns(n)] = jnp.transpose(ref[a, pl.ds(0, rows), pl.ds(0, width)])
            for h in range(heads):
                prob = s_ref[n, h] * inverse[h]
                p_ref[n, :, pl.ds(h * rows, rows)] = prob.astype(BF16)
                d_prob = dot(values, gt_ref[h])
                ds_ref[n, :, pl.ds(h * rows, rows)] = (prob * (d_prob - delta[h])).astype(BF16)
        return carried

    sweep(score_grads_step, 0)
    q_all = q_ref[...].reshape(heads * rows, width)
    g_all = g_ref[...].reshape(heads * rows, width)

    def key_grads_step(blocks, carried):
        for n, _, out_ref, a in blocks:
            out_ref[a, :, pl.ds(0, width)] = (dot(ds_ref[n], q_all) * factor).astype(BF16)
            out_ref[a, :, pl.ds(width, width)] = dot(p_ref[n], g_all).astype(BF16)
        return carried

    sweep(key_grads_step, 0)
    dsib_ref[(1 - core) * last] = jnp.zeros(dsib_ref.shape[1:], BF16)
    for h in range(heads):
        att_ref[h] = jnp.transpose(o_ref[h]).astype(BF16)
        score = ds_ref[:, :, pl.ds(h * rows, rows)].reshape(-1, rows)
        dq_ref[h] = (jnp.transpose(dot(kt_ref[...], score)) * factor).astype(BF16)


def arrange_kernel(*refs):
    for ref, out_ref in zip(refs[:2], refs[2:]):
        heads = [ref[h].astype(F32) for h in range(ref.shape[0])]
        out_ref[...] = jnp.stack(heads, axis=1).astype(BF16)


def attention(core, q, g, mine, sib):
    heads, rows, width = q.shape
    blocks = mine.shape[0]
    reach = 2 * blocks - 1
    vmem = pl.BlockSpec(memory_space=pltpu.VMEM)
    shape = jax.ShapeDtypeStruct
    return pl.pallas_call(
        attention_kernel,
        out_shape=(
            shape((heads, rows, width), BF16),
            shape((heads, rows, width), BF16),
            shape((blocks, rows, 2 * width), BF16),
            shape((blocks, rows, 2 * width), BF16),
        ),
        in_specs=[pl.BlockSpec(memory_space=pltpu.SMEM)] + [vmem] * 4,
        out_specs=(vmem,) * 4,
        scratch_shapes=[
            pltpu.VMEM((reach, heads, rows, rows), F32),
            pltpu.VMEM((reach, rows, heads * rows), BF16),
            pltpu.VMEM((reach, rows, heads * rows), BF16),
            pltpu.VMEM((heads, width, rows), F32),
            pltpu.VMEM((heads, width, rows), BF16),
            pltpu.VMEM((heads, width, rows), BF16),
            pltpu.VMEM((width, reach * rows), BF16),
            pltpu.VMEM((width, reach * rows), BF16),
        ],
        compiler_params=pltpu.CompilerParams(vmem_limit_bytes=32 * 1024 * 1024),
        name="attention",
    )(core, q, g, mine, sib)


def arrange(att, dq):
    heads, rows, width = att.shape
    vmem = pl.BlockSpec(memory_space=pltpu.VMEM)
    shape = jax.ShapeDtypeStruct((rows, heads, width), BF16)
    return pl.pallas_call(
        arrange_kernel,
        out_shape=(shape, shape),
        in_specs=[vmem] * 2,
        out_specs=(vmem,) * 2,
        compiler_params=pltpu.CompilerParams(vmem_limit_bytes=16 * 1024 * 1024),
        name="arrange",
    )(att, dq)


def per_device(queries, key_vectors, value_vectors, out_grad, doc_ids):
    rows, heads, width = queries.shape
    ctx_count = lax.axis_size("ctx")
    tp_count = lax.axis_size("tp")
    ctx_rank = lax.axis_index("ctx")
    tp_rank = lax.axis_index("tp")
    share = tp_count // KVH
    kv_head = tp_rank // share
    half = lax.rem(tp_rank, share)
    core = lax.rem(ctx_rank, 2).reshape(1)
    swap_core = [(i, i ^ 1) for i in range(ctx_count)]
    swap_half = [(i, i ^ 1) for i in range(tp_count)]

    def head_of(array):
        return lax.dynamic_slice_in_dim(array, kv_head, 1, 1).reshape(rows, width)

    doc_rows = jnp.broadcast_to((doc_ids + 1).astype(BF16)[None], (16, rows))
    pair = jnp.concatenate([head_of(key_vectors), head_of(value_vectors)], axis=1)
    own = jnp.concatenate([pair, doc_rows], axis=0)
    parts = [
        lax.ppermute(own, "ctx", [(i, i + 2 * d) for i in range(ctx_count - 2 * d)])
        for d in range(BACK, 0, -1)
    ]
    mine = jnp.stack(parts + [own])
    sib = lax.ppermute(mine, "ctx", swap_core)
    q = jnp.transpose(queries, (1, 0, 2))
    g = jnp.transpose(out_grad, (1, 0, 2))
    att, dq, d_mine, d_sib = attention(core, q, g, mine, sib)

    from_sib = lax.ppermute(d_sib, "ctx", swap_core)
    both = [(d_mine[a].astype(F32) + from_sib[a].astype(F32)) for a in range(BACK + 1)]
    total = both[BACK]
    for a in range(BACK):
        d = BACK - a
        total = total + lax.ppermute(
            both[a].astype(BF16), "ctx", [(i, i - 2 * d) for i in range(2 * d, ctx_count)]
        ).astype(F32)
    attended, query_grad = arrange(att, dq)
    total, attended, query_grad = lax.optimization_barrier((total, attended, query_grad))
    part = rows // share
    kept = lax.dynamic_slice_in_dim(total, half * part, part, 0)
    given = lax.dynamic_slice_in_dim(total, (1 - half) * part, part, 0).astype(BF16)
    final = (kept + lax.ppermute(given, "tp", swap_half).astype(F32)).astype(BF16)


    def along(block, d):
        return lax.ppermute(block, "tp", [(i, (i + share * d) % tp_count) for i in range(tp_count)])

    def across(block):
        return lax.ppermute(block, "tp", swap_half)

    before, after = along(final, 1), along(final, -1)
    close = jnp.stack([before, final, after])
    low, high = along(close[:2], 2), along(close[1:], -2)
    close_far = across(close)
    last = along(low[:1], 1)
    mid = jnp.concatenate([low, high])
    mid_far = across(mid)
    last_far = across(last)
    near = jnp.concatenate([last, low, close, high])
    far = jnp.concatenate([last_far, mid_far[:2], close_far, mid_far[2:]])
    near, far = (
        lax.dynamic_slice_in_dim(jnp.concatenate([x, x]), KVH - lax.rem(kv_head + 4, KVH), KVH, 0)
        for x in (near, far)
    )

    def merged(column):
        out = jnp.zeros((rows, KVH, width), BF16)
        for piece, place in ((near, half), (far, 1 - half)):
            piece = piece.reshape(KVH, part, 2 * width)[:, :, column * width : (column + 1) * width]
            out = lax.dynamic_update_slice_in_dim(
                out, jnp.transpose(piece, (1, 0, 2)), place * part, 0
            )
        return out

    return (
        attended,
        query_grad,
        merged(0),
        merged(1),
    )


def solution(mesh):
    return jax.shard_map(
        per_device,
        mesh=mesh,
        in_specs=(
            P("ctx", "tp", None),
            P("ctx", None, None),
            P("ctx", None, None),
            P("ctx", "tp", None),
            P("ctx"),
        ),
        out_specs=(
            P("ctx", "tp", None),
            P("ctx", "tp", None),
            P("ctx", None, None),
            P("ctx", None, None),
        ),
        check_vma=False,
    )
```

```python
import functools
import math

import jax
import jax.numpy as jnp
from jax import lax
from jax.experimental import pallas as pl
from jax.experimental.pallas import tpu as pltpu
from jax.sharding import PartitionSpec as P

KVH = 8
NEGATIVE = -1e30
BACK = 4
F32 = jnp.float32
BF16 = jnp.bfloat16


def dot(a, b, contract=(1, 0)):
    return lax.dot_general(a, b, ((contract[:1], contract[1:]), ((), ())), preferred_element_type=F32)


def attention_kernel(
    core_ref, q_ref, g_ref, mine_ref, sib_ref,
    att_ref, dq_ref, dmine_ref, dsib_ref,
    s_ref, p_ref, ds_ref, o_ref, qt_ref, gt_ref, kt_ref, vt_ref,
):
    heads, rows, width = q_ref.shape
    last = mine_ref.shape[0] - 1
    factor = 1.0 / math.sqrt(width)
    base2 = factor / math.log(2.0)
    core = core_ref[0]
    q_doc = mine_ref[last, pl.ds(rows, 16), :].astype(F32)[:1]
    for h in range(heads):
        qt_ref[h] = jnp.transpose(q_ref[h])
        gt_ref[h] = jnp.transpose(g_ref[h])

    def earlier(j):
        return (2 * j, mine_ref, dmine_ref, j), (2 * j + 1, sib_ref, dsib_ref, j + core)

    own = ((2 * last, mine_ref, dmine_ref, last),)

    def sweep(step, carried):
        for j in range(last):
            carried = step(earlier(j), carried)
        return step(own, carried)

    def columns(n):
        return pl.ds(n * rows, rows)

    def scores_step(blocks, peaks):
        peaks = list(peaks)
        for n, ref, _, a in blocks:
            keys = ref[a, pl.ds(0, rows), pl.ds(0, width)]
            k_doc = ref[a, pl.ds(rows, 16), :].astype(F32)[:1]
            k_col = jnp.transpose(jnp.broadcast_to(k_doc, (width, rows)))
            allowed = jnp.concatenate([k_col] * (rows // width), axis=1) == q_doc
            if blocks is own:
                allowed &= lax.broadcasted_iota(jnp.int32, (rows, rows), 0) <= (
                    lax.broadcasted_iota(jnp.int32, (rows, rows), 1)
                )
            for h in range(heads):
                raw = jnp.where(allowed, dot(keys, qt_ref[h]) * base2, NEGATIVE)
                s_ref[n, h] = raw
                peaks[h] = jnp.maximum(peaks[h], jnp.max(raw.reshape(rows // 8, 8, rows), axis=0))
        return tuple(peaks)

    peaks = sweep(scores_step, tuple(jnp.full((8, rows), NEGATIVE, F32) for _ in range(heads)))
    peak = [jnp.max(p, axis=0, keepdims=True) for p in peaks]

    def weights_step(blocks, masses):
        masses = list(masses)
        for n, ref, _, a in blocks:
            vt_ref[:, columns(n)] = jnp.transpose(ref[a, pl.ds(0, rows), pl.ds(width, width)])
            for h in range(heads):
                weights = jnp.exp2(s_ref[n, h] - peak[h])
                s_ref[n, h] = weights
                masses[h] = masses[h] + jnp.sum(weights.reshape(rows // 8, 8, rows), axis=0)
                p_ref[n, :, pl.ds(h * rows, rows)] = weights.astype(BF16)
        return tuple(masses)

    masses = sweep(weights_step, tuple(jnp.zeros((8, rows), F32) for _ in range(heads)))
    inverse, delta = [], []
    for h in range(heads):
        mass = jnp.sum(masses[h], axis=0, keepdims=True)
        inverse.append(1.0 / mass)
        weights = p_ref[:, :, pl.ds(h * rows, rows)].reshape(-1, rows)
        out = (dot(vt_ref[...], weights) / mass).astype(BF16).astype(F32)
        delta.append(jnp.sum(out * gt_ref[h].astype(F32), axis=0, keepdims=True))
        o_ref[h] = out

    def score_grads_step(blocks, carried):
        for n, ref, _, a in blocks:
            values = ref[a, pl.ds(0, rows), pl.ds(width, width)]
            kt_ref[:, columns(n)] = jnp.transpose(ref[a, pl.ds(0, rows), pl.ds(0, width)])
            for h in range(heads):
                prob = s_ref[n, h] * inverse[h]
                p_ref[n, :, pl.ds(h * rows, rows)] = prob.astype(BF16)
                d_prob = dot(values, gt_ref[h])
                ds_ref[n, :, pl.ds(h * rows, rows)] = (prob * (d_prob - delta[h])).astype(BF16)
        return carried

    sweep(score_grads_step, 0)
    q_all = q_ref[...].reshape(heads * rows, width)
    g_all = g_ref[...].reshape(heads * rows, width)

    def key_grads_step(blocks, carried):
        for n, _, out_ref, a in blocks:
            out_ref[a, :, pl.ds(0, width)] = (dot(ds_ref[n], q_all) * factor).astype(BF16)
            out_ref[a, :, pl.ds(width, width)] = dot(p_ref[n], g_all).astype(BF16)
        return carried

    sweep(key_grads_step, 0)
    dsib_ref[(1 - core) * last] = jnp.zeros(dsib_ref.shape[1:], BF16)
    for h in range(heads):
        att_ref[h] = jnp.transpose(o_ref[h]).astype(BF16)
        score = ds_ref[:, :, pl.ds(h * rows, rows)].reshape(-1, rows)
        dq_ref[h] = (jnp.transpose(dot(kt_ref[...], score)) * factor).astype(BF16)


def arrange_kernel(*refs):
    for ref, out_ref in zip(refs[:2], refs[2:]):
        heads = [ref[h].astype(F32) for h in range(ref.shape[0])]
        out_ref[...] = jnp.stack(heads, axis=1).astype(BF16)


def attention(core, q, g, mine, sib):
    heads, rows, width = q.shape
    blocks = mine.shape[0]
    reach = 2 * blocks - 1
    vmem = pl.BlockSpec(memory_space=pltpu.VMEM)
    shape = jax.ShapeDtypeStruct
    return pl.pallas_call(
        attention_kernel,
        out_shape=(
            shape((heads, rows, width), BF16),
            shape((heads, rows, width), BF16),
            shape((blocks, rows, 2 * width), BF16),
            shape((blocks, rows, 2 * width), BF16),
        ),
        in_specs=[pl.BlockSpec(memory_space=pltpu.SMEM)] + [vmem] * 4,
        out_specs=(vmem,) * 4,
        scratch_shapes=[
            pltpu.VMEM((reach, heads, rows, rows), F32),
            pltpu.VMEM((reach, rows, heads * rows), BF16),
            pltpu.VMEM((reach, rows, heads * rows), BF16),
            pltpu.VMEM((heads, width, rows), F32),
            pltpu.VMEM((heads, width, rows), BF16),
            pltpu.VMEM((heads, width, rows), BF16),
            pltpu.VMEM((width, reach * rows), BF16),
            pltpu.VMEM((width, reach * rows), BF16),
        ],
        compiler_params=pltpu.CompilerParams(vmem_limit_bytes=32 * 1024 * 1024),
        name="attention",
    )(core, q, g, mine, sib)


def arrange(att, dq):
    heads, rows, width = att.shape
    vmem = pl.BlockSpec(memory_space=pltpu.VMEM)
    shape = jax.ShapeDtypeStruct((rows, heads, width), BF16)
    return pl.pallas_call(
        arrange_kernel,
        out_shape=(shape, shape),
        in_specs=[vmem] * 2,
        out_specs=(vmem,) * 2,
        compiler_params=pltpu.CompilerParams(vmem_limit_bytes=16 * 1024 * 1024),
        name="arrange",
    )(att, dq)


def split_kernel(place_ref, mine_ref, sib_ref, *out_refs):
    rows = mine_ref.shape[1]
    x, line = place_ref[0], place_ref[1]
    for d, out_ref in enumerate(out_refs):
        goal = lax.rem(x + d, len(out_refs))
        part = out_ref.shape[1]
        tokens = pl.ds(pl.multiple_of(goal // 2 * part, part), part)
        for row in range(out_ref.shape[0]):
            a = 2 * row + lax.rem(goal, 2) - line
            held = (a >= 0) & (a < mine_ref.shape[0])
            a = jnp.clip(a, 0, mine_ref.shape[0] - 1)
            both = mine_ref[a, tokens, :].astype(F32) + sib_ref[a, tokens, :].astype(F32)
            out_ref[row] = jnp.where(held, both, 0.0).astype(BF16)


def split(place, mine, sib):
    blocks, rows, width = mine.shape
    vmem = pl.BlockSpec(memory_space=pltpu.VMEM)
    shape = jax.ShapeDtypeStruct(((blocks + 1) // 2, rows // 2, width), BF16)
    return pl.pallas_call(
        split_kernel,
        out_shape=(shape,) * 4,
        in_specs=[pl.BlockSpec(memory_space=pltpu.SMEM)] + [vmem] * 2,
        out_specs=(vmem,) * 4,
        compiler_params=pltpu.CompilerParams(vmem_limit_bytes=16 * 1024 * 1024),
        name="split",
    )(place, mine, sib)


def per_device(queries, key_vectors, value_vectors, out_grad, doc_ids):
    rows, heads, width = queries.shape
    ctx_count = lax.axis_size("ctx")
    tp_count = lax.axis_size("tp")
    ctx_rank = lax.axis_index("ctx")
    tp_rank = lax.axis_index("tp")
    share = tp_count // KVH
    kv_head = tp_rank // share
    half = lax.rem(tp_rank, share)
    core = lax.rem(ctx_rank, 2).reshape(1)
    swap_core = [(i, i ^ 1) for i in range(ctx_count)]
    swap_half = [(i, i ^ 1) for i in range(tp_count)]

    def head_of(array):
        return lax.dynamic_slice_in_dim(array, kv_head, 1, 1).reshape(rows, width)

    doc_rows = jnp.broadcast_to((doc_ids + 1).astype(BF16)[None], (16, rows))
    pair = jnp.concatenate([head_of(key_vectors), head_of(value_vectors)], axis=1)
    own = jnp.concatenate([pair, doc_rows], axis=0)
    parts = [
        lax.ppermute(own, "ctx", [(i, i + 2 * d) for i in range(ctx_count - 2 * d)])
        for d in range(BACK, 0, -1)
    ]
    mine = jnp.stack(parts + [own])
    sib = lax.ppermute(mine, "ctx", swap_core)
    q = jnp.transpose(queries, (1, 0, 2))
    g = jnp.transpose(out_grad, (1, 0, 2))
    att, dq, d_mine, d_sib = attention(core, q, g, mine, sib)

    from_sib = lax.ppermute(d_sib, "ctx", swap_core)
    line = lax.rem(ctx_rank // 2, 2)
    pieces = split(jnp.stack([2 * half + line, line]), d_mine, from_sib)

    def round_x(piece, d):
        pairs = []
        for c in range(ctx_count):
            for t in range(tp_count):
                goal = (2 * (t % 2) + c // 2 % 2 + d) % 4
                there = (c // 4 * 4 + goal % 2 * 2 + c % 2) * tp_count + t // 2 * 2 + goal // 2
                pairs.append((c * tp_count + t, there))
        return lax.ppermute(piece, ("ctx", "tp"), pairs)

    sums = pieces[0].astype(F32)
    for d in (1, 3, 2):
        sums = sums + round_x(pieces[d], d).astype(F32)
    attended, query_grad = arrange(att, dq)
    sums, attended, query_grad = lax.optimization_barrier((sums, attended, query_grad))
    total = sums[2]
    for row in (1, 0):
        d = 4 * (2 - row)
        total = total + lax.ppermute(
            sums[row].astype(BF16), "ctx", [(i, i - d) for i in range(d, ctx_count)]
        ).astype(F32)
    part = rows // share
    final = total.astype(BF16)

    def along(block, d):
        return lax.ppermute(block, "tp", [(i, (i + share * d) % tp_count) for i in range(tp_count)])

    def across(block):
        return lax.ppermute(block, "tp", swap_half)

    before, after = along(final, 1), along(final, -1)
    close = jnp.stack([before, final, after])
    low, high = along(close[:2], 2), along(close[1:], -2)
    close_far = across(close)
    last = along(low[:1], 1)
    mid = jnp.concatenate([low, high])
    mid_far = across(mid)
    last_far = across(last)
    near = jnp.concatenate([last, low, close, high])
    far = jnp.concatenate([last_far, mid_far[:2], close_far, mid_far[2:]])
    near, far = (
        lax.dynamic_slice_in_dim(jnp.concatenate([x, x]), KVH - lax.rem(kv_head + 4, KVH), KVH, 0)
        for x in (near, far)
    )

    def merged(column):
        out = jnp.zeros((rows, KVH, width), BF16)
        for piece, place in ((near, half), (far, 1 - half)):
            piece = piece.reshape(KVH, part, 2 * width)[:, :, column * width : (column + 1) * width]
            out = lax.dynamic_update_slice_in_dim(
                out, jnp.transpose(piece, (1, 0, 2)), place * part, 0
            )
        return out

    return (
        attended,
        query_grad,
        merged(0),
        merged(1),
    )


def solution(mesh):
    return jax.shard_map(
        per_device,
        mesh=mesh,
        in_specs=(
            P("ctx", "tp", None),
            P("ctx", None, None),
            P("ctx", None, None),
            P("ctx", "tp", None),
            P("ctx"),
        ),
        out_specs=(
            P("ctx", "tp", None),
            P("ctx", "tp", None),
            P("ctx", None, None),
            P("ctx", None, None),
        ),
        check_vma=False,
    )
```

```python
import functools
import math

import jax
import jax.numpy as jnp
from jax import lax
from jax.experimental import pallas as pl
from jax.experimental.pallas import tpu as pltpu
from jax.sharding import PartitionSpec as P

KVH = 8
NEGATIVE = -1e30
BACK = 4
F32 = jnp.float32
BF16 = jnp.bfloat16


def dot(a, b, contract=(1, 0)):
    return lax.dot_general(a, b, ((contract[:1], contract[1:]), ((), ())), preferred_element_type=F32)


def attention_kernel(
    core_ref, q_ref, g_ref, mine_ref, sib_ref,
    att_ref, dq_ref, dmine_ref, dsib_ref,
    s_ref, p_ref, ds_ref, o_ref, qt_ref, gt_ref, kt_ref, vt_ref,
):
    heads, rows, width = q_ref.shape
    last = mine_ref.shape[0] - 1
    factor = 1.0 / math.sqrt(width)
    base2 = factor / math.log(2.0)
    core = core_ref[0]
    q_doc = mine_ref[last, pl.ds(rows, 16), :].astype(F32)[:1]
    for h in range(heads):
        qt_ref[h] = jnp.transpose(q_ref[h])
        gt_ref[h] = jnp.transpose(g_ref[h])

    def earlier(j):
        return (2 * j, mine_ref, dmine_ref, j), (2 * j + 1, sib_ref, dsib_ref, j + core)

    own = ((2 * last, mine_ref, dmine_ref, last),)

    def sweep(step, carried):
        for j in range(last):
            carried = step(earlier(j), carried)
        return step(own, carried)

    def columns(n):
        return pl.ds(n * rows, rows)

    def scores_step(blocks, peaks):
        peaks = list(peaks)
        for n, ref, _, a in blocks:
            keys = ref[a, pl.ds(0, rows), pl.ds(0, width)]
            k_doc = ref[a, pl.ds(rows, 16), :].astype(F32)[:1]
            k_col = jnp.transpose(jnp.broadcast_to(k_doc, (width, rows)))
            allowed = jnp.concatenate([k_col] * (rows // width), axis=1) == q_doc
            if blocks is own:
                allowed &= lax.broadcasted_iota(jnp.int32, (rows, rows), 0) <= (
                    lax.broadcasted_iota(jnp.int32, (rows, rows), 1)
                )
            for h in range(heads):
                raw = jnp.where(allowed, dot(keys, qt_ref[h]) * base2, NEGATIVE)
                s_ref[n, h] = raw
                peaks[h] = jnp.maximum(peaks[h], jnp.max(raw.reshape(rows // 8, 8, rows), axis=0))
        return tuple(peaks)

    peaks = sweep(scores_step, tuple(jnp.full((8, rows), NEGATIVE, F32) for _ in range(heads)))
    peak = [jnp.max(p, axis=0, keepdims=True) for p in peaks]

    def weights_step(blocks, masses):
        masses = list(masses)
        for n, ref, _, a in blocks:
            vt_ref[:, columns(n)] = jnp.transpose(ref[a, pl.ds(0, rows), pl.ds(width, width)])
            for h in range(heads):
                weights = jnp.exp2(s_ref[n, h] - peak[h])
                s_ref[n, h] = weights
                masses[h] = masses[h] + jnp.sum(weights.reshape(rows // 8, 8, rows), axis=0)
                p_ref[n, :, pl.ds(h * rows, rows)] = weights.astype(BF16)
        return tuple(masses)

    masses = sweep(weights_step, tuple(jnp.zeros((8, rows), F32) for _ in range(heads)))
    inverse, delta = [], []
    for h in range(heads):
        mass = jnp.sum(masses[h], axis=0, keepdims=True)
        inverse.append(1.0 / mass)
        weights = p_ref[:, :, pl.ds(h * rows, rows)].reshape(-1, rows)
        out = (dot(vt_ref[...], weights) / mass).astype(BF16).astype(F32)
        delta.append(jnp.sum(out * gt_ref[h].astype(F32), axis=0, keepdims=True))
        o_ref[h] = out

    def score_grads_step(blocks, carried):
        for n, ref, _, a in blocks:
            values = ref[a, pl.ds(0, rows), pl.ds(width, width)]
            kt_ref[:, columns(n)] = jnp.transpose(ref[a, pl.ds(0, rows), pl.ds(0, width)])
            for h in range(heads):
                prob = s_ref[n, h] * inverse[h]
                p_ref[n, :, pl.ds(h * rows, rows)] = prob.astype(BF16)
                d_prob = dot(values, gt_ref[h])
                ds_ref[n, :, pl.ds(h * rows, rows)] = (prob * (d_prob - delta[h])).astype(BF16)
        return carried

    sweep(score_grads_step, 0)
    q_all = q_ref[...].reshape(heads * rows, width)
    g_all = g_ref[...].reshape(heads * rows, width)

    def key_grads_step(blocks, carried):
        first, count = blocks[0][0], len(blocks)
        shape = (count * rows, heads * rows)
        d_keys = dot(ds_ref[pl.ds(first, count)].reshape(shape), q_all) * factor
        d_values = dot(p_ref[pl.ds(first, count)].reshape(shape), g_all)
        for i, (_, _, out_ref, a) in enumerate(blocks):
            out_ref[a, :, pl.ds(0, width)] = d_keys[i * rows : (i + 1) * rows].astype(BF16)
            out_ref[a, :, pl.ds(width, width)] = d_values[i * rows : (i + 1) * rows].astype(BF16)
        return carried

    sweep(key_grads_step, 0)
    dsib_ref[(1 - core) * last] = jnp.zeros(dsib_ref.shape[1:], BF16)
    for h in range(heads):
        att_ref[h] = jnp.transpose(o_ref[h]).astype(BF16)
        score = ds_ref[:, :, pl.ds(h * rows, rows)].reshape(-1, rows)
        dq_ref[h] = (jnp.transpose(dot(kt_ref[...], score)) * factor).astype(BF16)


def arrange_kernel(*refs):
    for ref, out_ref in zip(refs[:2], refs[2:]):
        heads = [ref[h].astype(F32) for h in range(ref.shape[0])]
        out_ref[...] = jnp.stack(heads, axis=1).astype(BF16)


def attention(core, q, g, mine, sib):
    heads, rows, width = q.shape
    blocks = mine.shape[0]
    reach = 2 * blocks - 1
    vmem = pl.BlockSpec(memory_space=pltpu.VMEM)
    shape = jax.ShapeDtypeStruct
    return pl.pallas_call(
        attention_kernel,
        out_shape=(
            shape((heads, rows, width), BF16),
            shape((heads, rows, width), BF16),
            shape((blocks, rows, 2 * width), BF16),
            shape((blocks, rows, 2 * width), BF16),
        ),
        in_specs=[pl.BlockSpec(memory_space=pltpu.SMEM)] + [vmem] * 4,
        out_specs=(vmem,) * 4,
        scratch_shapes=[
            pltpu.VMEM((reach, heads, rows, rows), F32),
            pltpu.VMEM((reach, rows, heads * rows), BF16),
            pltpu.VMEM((reach, rows, heads * rows), BF16),
            pltpu.VMEM((heads, width, rows), F32),
            pltpu.VMEM((heads, width, rows), BF16),
            pltpu.VMEM((heads, width, rows), BF16),
            pltpu.VMEM((width, reach * rows), BF16),
            pltpu.VMEM((width, reach * rows), BF16),
        ],
        compiler_params=pltpu.CompilerParams(vmem_limit_bytes=32 * 1024 * 1024),
        name="attention",
    )(core, q, g, mine, sib)


def arrange(att, dq):
    heads, rows, width = att.shape
    vmem = pl.BlockSpec(memory_space=pltpu.VMEM)
    shape = jax.ShapeDtypeStruct((rows, heads, width), BF16)
    return pl.pallas_call(
        arrange_kernel,
        out_shape=(shape, shape),
        in_specs=[vmem] * 2,
        out_specs=(vmem,) * 2,
        compiler_params=pltpu.CompilerParams(vmem_limit_bytes=16 * 1024 * 1024),
        name="arrange",
    )(att, dq)


def per_device(queries, key_vectors, value_vectors, out_grad, doc_ids):
    rows, heads, width = queries.shape
    ctx_count = lax.axis_size("ctx")
    tp_count = lax.axis_size("tp")
    ctx_rank = lax.axis_index("ctx")
    tp_rank = lax.axis_index("tp")
    share = tp_count // KVH
    kv_head = tp_rank // share
    half = lax.rem(tp_rank, share)
    core = lax.rem(ctx_rank, 2).reshape(1)
    swap_core = [(i, i ^ 1) for i in range(ctx_count)]
    swap_half = [(i, i ^ 1) for i in range(tp_count)]

    def head_of(array):
        return lax.dynamic_slice_in_dim(array, kv_head, 1, 1).reshape(rows, width)

    doc_rows = jnp.broadcast_to((doc_ids + 1).astype(BF16)[None], (16, rows))
    pair = jnp.concatenate([head_of(key_vectors), head_of(value_vectors)], axis=1)
    own = jnp.concatenate([pair, doc_rows], axis=0)
    parts = [
        lax.ppermute(own, "ctx", [(i, i + 2 * d) for i in range(ctx_count - 2 * d)])
        for d in range(BACK, 0, -1)
    ]
    mine = jnp.stack(parts + [own])
    sib = lax.ppermute(mine, "ctx", swap_core)
    q = jnp.transpose(queries, (1, 0, 2))
    g = jnp.transpose(out_grad, (1, 0, 2))
    att, dq, d_mine, d_sib = attention(core, q, g, mine, sib)

    from_sib = lax.ppermute(d_sib, "ctx", swap_core)
    line = lax.rem(ctx_rank // 2, 2)
    blank = jnp.zeros((1, rows, 2 * width), BF16)
    both = (d_mine.astype(F32) + from_sib.astype(F32)).astype(BF16)
    slots = lax.dynamic_slice_in_dim(jnp.concatenate([blank, both, blank]), 1 - line, BACK + 2, 0)
    slots = slots.reshape(BACK // 2 + 1, 2, share, rows // share, 2 * width)

    def piece_for(d):
        goal = lax.rem(2 * half + line + d, 4)
        piece = lax.dynamic_slice_in_dim(slots, lax.rem(goal, 2), 1, 1)
        return lax.dynamic_slice_in_dim(piece, goal // 2, 1, 2)[:, 0, 0]

    pieces = [piece_for(d) for d in range(4)]

    def round_x(piece, d):
        pairs = []
        for c in range(ctx_count):
            for t in range(tp_count):
                goal = (2 * (t % 2) + c // 2 % 2 + d) % 4
                there = (c // 4 * 4 + goal % 2 * 2 + c % 2) * tp_count + t // 2 * 2 + goal // 2
                pairs.append((c * tp_count + t, there))
        return lax.ppermute(piece, ("ctx", "tp"), pairs)

    sums = pieces[0].astype(F32)
    for d in (1, 3, 2):
        sums = sums + round_x(pieces[d], d).astype(F32)
    attended, query_grad = arrange(att, dq)
    sums, attended, query_grad = lax.optimization_barrier((sums, attended, query_grad))
    total = sums[2]
    for row in (1, 0):
        d = 4 * (2 - row)
        total = total + lax.ppermute(
            sums[row].astype(BF16), "ctx", [(i, i - d) for i in range(d, ctx_count)]
        ).astype(F32)
    part = rows // share
    final = total.astype(BF16)

    def along(block, d):
        return lax.ppermute(block, "tp", [(i, (i + share * d) % tp_count) for i in range(tp_count)])

    def across(block):
        return lax.ppermute(block, "tp", swap_half)

    before, after = along(final, 1), along(final, -1)
    close = jnp.stack([before, final, after])
    low, high = along(close[:2], 2), along(close[1:], -2)
    close_far = across(close)
    last = along(low[:1], 1)
    mid = jnp.concatenate([low, high])
    mid_far = across(mid)
    last_far = across(last)
    near = jnp.concatenate([last, low, close, high])
    far = jnp.concatenate([last_far, mid_far[:2], close_far, mid_far[2:]])
    near, far = (
        lax.dynamic_slice_in_dim(jnp.concatenate([x, x]), KVH - lax.rem(kv_head + 4, KVH), KVH, 0)
        for x in (near, far)
    )

    def merged(column):
        out = jnp.zeros((rows, KVH, width), BF16)
        for piece, place in ((near, half), (far, 1 - half)):
            piece = piece.reshape(KVH, part, 2 * width)[:, :, column * width : (column + 1) * width]
            out = lax.dynamic_update_slice_in_dim(
                out, jnp.transpose(piece, (1, 0, 2)), place * part, 0
            )
        return out

    return (
        attended,
        query_grad,
        merged(0),
        merged(1),
    )


def solution(mesh):
    return jax.shard_map(
        per_device,
        mesh=mesh,
        in_specs=(
            P("ctx", "tp", None),
            P("ctx", None, None),
            P("ctx", None, None),
            P("ctx", "tp", None),
            P("ctx"),
        ),
        out_specs=(
            P("ctx", "tp", None),
            P("ctx", "tp", None),
            P("ctx", None, None),
            P("ctx", None, None),
        ),
        check_vma=False,
    )
```
